32 devices in a mesh: lon: 8 (over z, x), lat: 4 (over y, core).
Axes of the slice: x: 2, y: 2, z: 4, core: 2. Of those that a mesh axis runs over, the one named last changes fastest.
Arguments:
- elevation: float32 [12, 384, 1024], P(None, 'lat', 'lon'), may hold values from -6 to 6
- equilibrium: float32 [12, 384, 1024], P(None, 'lat', 'lon'), may hold values from -4 to 4
- transport_u: float32 [12, 384, 1024], P(None, 'lat', 'lon'), may hold values from -4 to 4
- transport_v: float32 [12, 384, 1024], P(None, 'lat', 'lon'), may hold values from -4 to 4
- ocean_depth: float32 [384, 1024], P('lat', 'lon'), may hold values from 0.3 to 3
- bottom_drag: float32 [384, 1024], P('lat', 'lon'), may hold values from 0.2 to 2
- wet_mask: int32 [384, 1024], P('lat', 'lon'), may hold values 0 or 1
- lon_green: float32 [1024, 128], P('lon'), may hold values from -0.5 to 0.5
- lat_green: float32 [384, 3072], P('lat', 'lon'), may hold values from -0.109375 to 0.109375
Outputs:
- elevation_next: float32 [12, 384, 1024], P(None, 'lat', 'lon')
- transport_u_next: float32 [12, 384, 1024], P(None, 'lat', 'lon')
- transport_v_next: float32 [12, 384, 1024], P(None, 'lat', 'lon')
The draws below stay inside these ranges and needn't reach their ends.
All inputs are finite; a program needn't handle non-finite values. No bound on the sum of `wet_mask` on one device may be relied on, other than what follows from the above.
Results may differ from the reference program's by a relative error of at most 0.0001.
Values sent between devices are 32-bit elements; how exact they have to be, the bound alone decides.
A program may use at most 64 MiB of HBM per device.

```python
import math
import jax
import jax.numpy as jnp
from jax import lax

COLUMNS = 12
TX = 128
NLAT = 384
NLON = 1024
N_LON = 8


def touch_ends(result, own_key, low, largest):
    place = [jax.random.randint(jax.random.fold_in(own_key, axis), (), 0, length) for axis, length in enumerate(result.shape)]
    longest = result.shape.index(max(result.shape))
    beside = place[:longest] + [(place[longest] + 1) % result.shape[longest]] + place[longest + 1:]
    return result.at[tuple(place)].set(low).at[tuple(beside)].set(largest)


def shard_levels(stream_key, shape, split, least, high):
    level = 1.0
    for position, shards_of in split:
        draws = jax.random.uniform(jax.random.fold_in(jax.random.fold_in(stream_key, 6), position), (shards_of,), jnp.float32, least / len(split), high / len(split))
        level = level * jnp.repeat(jnp.exp(draws), shape[position] // shards_of).reshape((-1,) + (1,) * (len(shape) - 1 - position))
    return level


def bell_draw(own_key, shape, scale, reach, cuts=(), kind=jnp.bfloat16):
    drawn = jax.random.normal(own_key, shape, jnp.float32) * scale
    if len(cuts) > 0:
        drawn = shard_levels(own_key, shape, cuts, -0.22, 0.18) * drawn
    return jnp.clip(drawn, min=-reach, max=reach).astype(kind)


def setup_inputs(seed: int = 0) -> dict:
    arg_keys = jax.random.split(jax.random.key(seed), 10)
    return {
        "elevation": bell_draw(arg_keys[0], (COLUMNS, NLAT, NLON), 1.0, 6.0, ((1, 4), (2, 8)), jnp.float32),
        "equilibrium": bell_draw(arg_keys[1], (COLUMNS, NLAT, NLON), 0.5, 4.0, ((1, 4), (2, 8)), jnp.float32),
        "transport_u": bell_draw(arg_keys[2], (COLUMNS, NLAT, NLON), 0.5, 4.0, ((1, 4), (2, 8)), jnp.float32),
        "transport_v": bell_draw(arg_keys[3], (COLUMNS, NLAT, NLON), 0.5, 4.0, ((1, 4), (2, 8)), jnp.float32),
        "ocean_depth": jnp.clip(jnp.exp(math.log(3.0) - 2.3025851 * jax.random.uniform(arg_keys[4], (NLAT, NLON), jnp.float32) ** shard_levels(arg_keys[4], (NLAT, NLON), ((0, 4), (1, 8)), -0.2, 0.2)), 0.3, 3.0),
        "bottom_drag": jnp.clip(jnp.exp(math.log(2.0) - 2.3025851 * jax.random.uniform(arg_keys[5], (NLAT, NLON), jnp.float32) ** shard_levels(arg_keys[5], (NLAT, NLON), ((0, 4), (1, 8)), -0.2, 0.2)), 0.2, 2.0),
        "wet_mask": touch_ends((jax.random.randint(arg_keys[6], (NLAT, NLON), 0, 10) < 7).astype(jnp.int32), jax.random.fold_in(arg_keys[6], 1), 0, 1),
        "lon_green": bell_draw(arg_keys[7], (NLON, TX), TX ** -0.5, 0.5, ((0, 8),), jnp.float32),
        "lat_green": bell_draw(arg_keys[8], (NLAT, NLAT * N_LON), (9 * NLAT) ** -0.5, 0.109375, ((0, 4), (1, 8)), jnp.float32),
    }


FREQS = [1.9323, 2.0, 1.8960, 2.0055, 1.0027, 0.9295]
VISCOSITY = 0.5


def row_terms(rows, nlat):
    angle = (-80.0 + 160.0 * (rows.astype(jnp.float32) + 0.5) / nlat) * (math.pi / 180.0)
    return (1.0 / jnp.cos(angle))[:, None], (2.0 * jnp.sin(angle))[:, None]


def extend_full(field, width):
    field = jnp.concatenate([field[:, :, -width:], field, field[:, :, :width]], axis=2)
    return jnp.pad(field, ((0, 0), (width, width), (0, 0)))


def slopes(potential_ext, stretch):
    east_slope = (potential_ext[:, 1:-1, 2:] - potential_ext[:, 1:-1, :-2]) * 0.5 * stretch
    north_slope = (potential_ext[:, 2:, 1:-1] - potential_ext[:, :-2, 1:-1]) * 0.5
    return east_slope, north_slope


def solve_cells(push_u, push_v, depth_field, drag_field, wet_frac, coriolis):
    damping = drag_field + 4.0 * VISCOSITY
    frequency = jnp.array(FREQS, jnp.float32)[:, None, None]
    det_real = damping * damping - frequency * frequency + coriolis * coriolis
    det_imag = 2.0 * damping * frequency
    magnitude = det_real * det_real + det_imag * det_imag

    def combine(first, second, factor):
        top_real = damping * first[:6] - frequency * first[6:] + factor * coriolis * second[:6]
        top_imag = damping * first[6:] + frequency * first[:6] + factor * coriolis * second[6:]
        out_real = (top_real * det_real + top_imag * det_imag) / magnitude
        out_imag = (top_imag * det_real - top_real * det_imag) / magnitude
        return wet_frac * jnp.concatenate([out_real, out_imag], axis=0)

    return jnp.concatenate([combine(push_u, push_v, 1.0), combine(push_v, push_u, -1.0)], axis=0)


def relax(flow_ext, east_slope, north_slope, depth_field, drag_field, wet_frac, coriolis):
    beside_all = flow_ext[:, :-2, 1:-1] + flow_ext[:, 2:, 1:-1] + flow_ext[:, 1:-1, :-2] + flow_ext[:, 1:-1, 2:]
    push_u = -depth_field * east_slope + VISCOSITY * beside_all[:12]
    push_v = -depth_field * north_slope + VISCOSITY * beside_all[12:]
    return solve_cells(push_u, push_v, depth_field, drag_field, wet_frac, coriolis)


def surface(east_ext, north_ext, stretch, wet_frac):
    spread = (east_ext[:, :, 2:] - east_ext[:, :, :-2]) * 0.5 * stretch + (north_ext[:, 2:, :] - north_ext[:, :-2, :]) * 0.5
    frequency = jnp.array(FREQS, jnp.float32)[:, None, None]
    return wet_frac * jnp.concatenate([-spread[6:] / frequency, spread[:6] / frequency], axis=0)


def reference(elevation, equilibrium, transport_u, transport_v, ocean_depth, bottom_drag, wet_mask, lon_green, lat_green):
    wet_frac = wet_mask.astype(jnp.float32)
    source = wet_frac * elevation
    blocks = source.reshape(12, NLAT, N_LON, TX)
    lon_blocks = lon_green.reshape(N_LON, TX, TX)
    mixed = jnp.einsum('krbj,bcj->krbc', blocks, lon_blocks, precision=lax.Precision.HIGHEST)
    lat_blocks = lat_green.reshape(NLAT, N_LON, NLAT)
    sal = jnp.einsum('rbs,ksbc->krbc', lat_blocks, mixed, precision=lax.Precision.HIGHEST).reshape(12, NLAT, NLON)
    potential = elevation - equilibrium - sal
    stretch, coriolis = row_terms(jnp.arange(NLAT), NLAT)
    east_slope, north_slope = slopes(extend_full(potential, 1), stretch)
    flows = jnp.concatenate([transport_u, transport_v], axis=0)
    for sweep_index in range(2):
        flows = relax(extend_full(flows, 1), east_slope, north_slope, ocean_depth, bottom_drag, wet_frac, coriolis)
    widened = extend_full(flows, 1)
    elevation_next = surface(widened[:12, 1:-1, :], widened[12:, :, 1:-1], stretch, wet_frac)
    return elevation_next, flows[:12], flows[12:]
```

```python
import functools
import math

import jax
import jax.numpy as jnp
from jax import lax
from jax.experimental import pallas as pl
from jax.experimental.pallas import tpu as pltpu
from jax.sharding import PartitionSpec as P

FREQS = [1.9323, 2.0, 1.896, 2.0055, 1.0027, 0.9295]
MESH = pl.DeviceIdType.MESH
HIGH = lax.Precision.HIGHEST
TOP = 16
HALO = 8
BLOCK = 16
STATICS = (36, 37, 38)
FIELDS = tuple(range(24)) + STATICS


def freq_of(j):
    w = jnp.float32(FREQS[0])
    for i in range(1, 6):
        w = jnp.where(j == i, jnp.float32(FREQS[i]), w)
    return w


def kernel(
    n_lat, n_lon, rows,
    elev_h, equil_h, u_h, v_h, dep_h, drag_h, mask_h, lon_h, lat_h,
    oe_h, ou_h, ov_h,
    elev_v, equil_v, mask_v, lon_v, lg, f, fs, mid, mids, two, twos, co, cos, tt, g,
    geo, x0, zl0, zr0, xp, zlp, zrp, eo,
    load_sem, g_send, g_recv, f_send, f_recv, a_send, a_recv, b_send, b_recv, p_send, p_recv, o_sem,
):
    total = n_lat * rows
    end = TOP + rows
    lo, hi = TOP - HALO, end + HALO
    blocks = (hi - lo) // BLOCK
    lat = lax.axis_index("lat")
    lon = lax.axis_index("lon")
    core, chip = lax.rem(lat, 2), lat // 2
    chips = n_lat // 2
    sib = lat + 1 - 2 * core
    right, left = lax.rem(lon + 1, n_lon), lax.rem(lon + n_lon - 1, n_lon)

    loads = [
        (elev_h, elev_v), (mask_h, mask_v), (equil_h, equil_v),
        (u_h, f.at[0:12, TOP:end]), (v_h, f.at[12:24, TOP:end]),
        (dep_h, f.at[36, TOP:end]), (drag_h, f.at[37, TOP:end]),
        (lat_h, lg.at[TOP:end]), (lon_h, lon_v),
    ]
    loads = [pltpu.make_async_copy(s, d, load_sem.at[i]) for i, (s, d) in enumerate(loads)]
    for c in loads:
        c.start()

    barrier = pltpu.get_barrier_semaphore()
    for d in range(1, n_lat):
        pl.semaphore_signal(barrier, inc=1, device_id={"lat": lax.rem(lat + d, n_lat)}, device_id_type=MESH)
    for side in (left, right):
        pl.semaphore_signal(barrier, inc=1, device_id={"lon": side}, device_id_type=MESH)

    own = pl.ds(pl.multiple_of(lat * rows, 8), rows)
    loads[0].wait()
    loads[1].wait()
    f[38, TOP:end] = mask_v[...].astype(jnp.float32)

    def make_source(j, _):
        wet = f[38, TOP:end]
        g[j, own, 0:128] = wet * elev_v[j]
        g[j, own, 128:256] = wet * elev_v[j + 6]
        return 0

    lax.fori_loop(0, 6, make_source, 0)
    pl.semaphore_wait(barrier, n_lat + 1)

    def remote(src, dst, ss, rs, where):
        return pltpu.make_async_remote_copy(
            src_ref=src, dst_ref=dst, send_sem=ss, recv_sem=rs, device_id=where, device_id_type=MESH)

    def block_of(d):
        return pl.ds(pl.multiple_of((lax.rem(chip + chips - d, chips) * 2 + core) * rows, 8), rows)

    def gather_copy(j, d):
        where = sib if d == 0 else lax.rem(chip + d, chips) * 2 + core
        return remote(g.at[j, own], g.at[j, own], g_send.at[j, d], g_recv.at[j, d], {"lat": where})

    def forward_copy(j, d):
        rows_d = block_of(d)
        return remote(g.at[j, rows_d], g.at[j, rows_d], f_send.at[j, d - 1], f_recv.at[j, d - 1], {"lat": sib})

    def start_gather(j, _):
        for d in range(1, chips):
            gather_copy(j, d).start()
        gather_copy(j, 0).start()
        return 0

    lax.fori_loop(0, 2, start_gather, 0)

    for c in loads[2:]:
        c.wait()

    def make_gap(k, _):
        f[24 + k, TOP:end] = elev_v[k] - equil_v[k]
        return 0

    lax.fori_loop(0, 12, make_gap, 0)

    up = [remote(f.at[:, TOP:TOP + HALO], f.at[:, end:hi], a_send.at[0], a_recv.at[0], {"lat": lax.max(lat - 1, 0)}),
          remote(lg.at[TOP:TOP + HALO], lg.at[end:hi], a_send.at[1], a_recv.at[1], {"lat": lax.max(lat - 1, 0)})]
    down = [remote(f.at[:, end - HALO:end], f.at[:, lo:TOP], a_send.at[2], a_recv.at[2], {"lat": lax.min(lat + 1, n_lat - 1)}),
            remote(lg.at[end - HALO:end], lg.at[lo:TOP], a_send.at[3], a_recv.at[3], {"lat": lax.min(lat + 1, n_lat - 1)})]

    @pl.when(lat > 0)
    def _():
        for c in up:
            c.start()

    @pl.when(lat < n_lat - 1)
    def _():
        for c in down:
            c.start()

    lax.fori_loop(2, 6, start_gather, 0)

    @pl.when(lat == 0)
    def _():
        f[:, lo:TOP] = jnp.zeros((39, HALO, 128), jnp.float32)
        lg[lo:TOP] = jnp.zeros((HALO, total), jnp.float32)

    @pl.when(lat == n_lat - 1)
    def _():
        f[:, end:hi] = jnp.zeros((39, HALO, 128), jnp.float32)
        lg[end:hi] = jnp.zeros((HALO, total), jnp.float32)

    row = lax.broadcasted_iota(jnp.int32, (hi + HALO, 128), 0) + (lat * rows - TOP)
    angle = (-80.0 + 160.0 * (row.astype(jnp.float32) + 0.5) / total) * (math.pi / 180.0)
    geo[0] = 1.0 / jnp.cos(angle)
    geo[1] = 2.0 * jnp.sin(angle)

    @pl.when(lat > 0)
    def _():
        for c in up:
            c.wait_send()
        for c in down:
            c.wait_recv()

    @pl.when(lat < n_lat - 1)
    def _():
        for c in down:
            c.wait_send()
        for c in up:
            c.wait_recv()

    lane = lax.broadcasted_iota(jnp.int32, (BLOCK, 128), 1)
    shifted = lax.rem(lane + 124, 128)
    window = shifted // 8
    from_left = lax.rem(shifted, 8) < 4

    def pack(pieces):
        packed = jnp.zeros((BLOCK, 128), jnp.float32)
        for pos, piece in enumerate(pieces):
            shift = (8 * pos + 8) % 128
            rolled = pltpu.roll(piece, shift, 1) if shift else piece
            packed = jnp.where(window == pos, rolled, packed)
        return packed

    def unpack(z, pos):
        shift = (128 - (8 * pos + 8)) % 128
        return pltpu.roll(z, shift, 1) if shift else z

    slots = [(fi, b) for fi in FIELDS for b in range(blocks)]
    tiles = -(-len(slots) // 16)
    for t in range(tiles):
        part = slots[16 * t:16 * t + 16]
        x0[t] = pack([f[fi, lo + BLOCK * b:lo + BLOCK * b + BLOCK] for fi, b in part])
    edge = [remote(x0, zl0, b_send.at[0], b_recv.at[0], {"lon": right}),
            remote(x0, zr0, b_send.at[1], b_recv.at[1], {"lon": left})]
    for c in edge:
        c.start()

    def coefficients(fields, coefs, j):
        w = freq_of(j)
        for b in range(blocks):
            rs = slice(lo + BLOCK * b, lo + BLOCK * b + BLOCK)
            d = fields[37, rs] + 2.0
            c = geo[1, rs]
            det_r = d * d - w * w + c * c
            det_i = 2.0 * d * w
            inv = fields[38, rs] * 0.5 / (det_r * det_r + det_i * det_i)
            coefs[4 * j, rs] = (d * det_r + w * det_i) * inv
            coefs[4 * j + 1, rs] = (w * det_r - d * det_i) * inv
            coefs[4 * j + 2, rs] = c * det_r * inv
            coefs[4 * j + 3, rs] = -c * det_i * inv

    def coef_main(j, _):
        coefficients(f, co, j)
        return 0

    def coef_side(j, _):
        coefficients(fs, cos, j)
        return 0

    lax.fori_loop(0, 6, coef_main, 0)
    for c in edge:
        c.wait()
    for t in range(tiles):
        z = jnp.where(from_left, zl0[t], zr0[t])
        for pos, (fi, b) in enumerate(slots[16 * t:16 * t + 16]):
            fs[fi, lo + BLOCK * b:lo + BLOCK * b + BLOCK] = unpack(z, pos)
    lax.fori_loop(0, 6, coef_side, 0)

    first_lane, last_lane = lane == 0, lane == 127

    def strips(j):
        return [remote(xp.at[j], zlp.at[j], p_send.at[j, 0], p_recv.at[j, 0], {"lon": right}),
                remote(xp.at[j], zrp.at[j], p_send.at[j, 1], p_recv.at[j, 1], {"lon": left})]

    def outs(j):
        copies = []
        for part in range(2):
            k = j + 6 * part
            copies += [
                pltpu.make_async_copy(eo.at[k], oe_h.at[k], o_sem.at[j, 3 * part]),
                pltpu.make_async_copy(two.at[k, TOP:end], ou_h.at[k], o_sem.at[j, 3 * part + 1]),
                pltpu.make_async_copy(two.at[12 + k, TOP:end], ov_h.at[k], o_sem.at[j, 3 * part + 2]),
            ]
        return copies

    def loading(j):
        for d in range(1, chips):
            gather_copy(j, d).wait_recv()
            forward_copy(j, d).start()
        gather_copy(j, 0).wait_recv()
        for d in range(1, chips):
            forward_copy(j, d).wait_recv()
        both = jnp.dot(lg[lo:hi], g[j], precision=HIGH, preferred_element_type=jnp.float32)
        for part in range(2):
            k = 24 + j + 6 * part
            sal = lax.dot_general(
                both[:, 128 * part:128 * part + 128], lon_v[...], (((1,), (1,)), ((), ())),
                precision=HIGH, preferred_element_type=jnp.float32)
            f[k, lo:hi] = f[k, lo:hi] - sal
        xp[j] = pack([
            f[24 + j + 6 * part, lo + BLOCK * b:lo + BLOCK * b + BLOCK]
            for part in range(2) for b in range(blocks)])
        for c in strips(j):
            c.start()

    def east_west(m, s):
        em, es = pltpu.roll(m, 127, 1), pltpu.roll(s, 127, 1)
        wm, ws = pltpu.roll(m, 1, 1), pltpu.roll(s, 1, 1)
        return (jnp.where(last_lane, es, em), jnp.where(last_lane, em, es),
                jnp.where(first_lane, ws, wm), jnp.where(first_lane, wm, ws))

    def relax(src, srcs, dst, dsts, j, b, side_v):
        r0 = lo + BLOCK * b
        rs, rn, ro = slice(r0, r0 + BLOCK), slice(r0 + 1, r0 + 1 + BLOCK), slice(r0 - 1, r0 - 1 + BLOCK)
        pm, ps = [], []
        for i in range(4):
            k = j + 6 * i
            em, es, wm, ws = east_west(src[k, rs], srcs[k, rs])
            pm.append(tt[i, rs] + (em + wm + src[k, rn] + src[k, ro]))
            ps.append(tt[4 + i, rs] + (es + ws + srcs[k, rn] + srcs[k, ro]))
        for push, coefs, to, with_v in ((pm, co, dst, True), (ps, cos, dsts, side_v)):
            ar, ai, br, bi = (coefs[4 * j + i, rs] for i in range(4))
            ur, ui, vr, vi = push
            to[j, rs] = ar * ur - ai * ui + br * vr - bi * vi
            to[j + 6, rs] = ar * ui + ai * ur + br * vi + bi * vr
            if with_v:
                to[j + 12, rs] = ar * vr - ai * vi - br * ur + bi * ui
                to[j + 18, rs] = ar * vi + ai * vr - br * ui - bi * ur

    def finish(j):
        for c in strips(j):
            c.wait()
        z = jnp.where(from_left, zlp[j], zrp[j])
        for part in range(2):
            for b in range(blocks):
                fs[24 + j + 6 * part, lo + BLOCK * b:lo + BLOCK * b + BLOCK] = unpack(z, part * blocks + b)
        for b in range(blocks):
            r0 = lo + BLOCK * b
            rs, rn, ro = slice(r0, r0 + BLOCK), slice(r0 + 1, r0 + 1 + BLOCK), slice(r0 - 1, r0 - 1 + BLOCK)
            stretch = geo[0, rs]
            dm, ds = f[36, rs], fs[36, rs]
            for part in range(2):
                k = 24 + j + 6 * part
                em, es, wm, ws = east_west(f[k, rs], fs[k, rs])
                tt[part, rs] = dm * stretch * (wm - em)
                tt[4 + part, rs] = ds * stretch * (ws - es)
                tt[2 + part, rs] = dm * (f[k, ro] - f[k, rn])
                tt[6 + part, rs] = ds * (fs[k, ro] - fs[k, rn])
        for b in range(blocks):
            relax(f, fs, mid, mids, j, b, True)
        for b in range(blocks):
            relax(mid, mids, two, twos, j, b, False)
        scale = 0.5 / freq_of(j)
        for b in range(rows // BLOCK):
            r0 = TOP + BLOCK * b
            rs, rn, ro = slice(r0, r0 + BLOCK), slice(r0 + 1, r0 + 1 + BLOCK), slice(r0 - 1, r0 - 1 + BLOCK)
            stretch = geo[0, rs]
            wet = f[38, rs] * scale
            spread = []
            for part in range(2):
                k = j + 6 * part
                em, _, wm, _ = east_west(two[k, rs], twos[k, rs])
                spread.append((em - wm) * stretch + (two[12 + k, rn] - two[12 + k, ro]))
            eo[j, BLOCK * b:BLOCK * b + BLOCK] = -wet * spread[1]
            eo[j + 6, BLOCK * b:BLOCK * b + BLOCK] = wet * spread[0]
        for c in outs(j):
            c.start()

    def step(j, _):
        @pl.when(j < 6)
        def _():
            loading(lax.min(j, 5))

        @pl.when(j > 0)
        def _():
            finish(lax.max(j - 1, 0))

        return 0

    lax.fori_loop(0, 7, step, 0)

    def drain(j, _):
        for c in outs(j):
            c.wait()
        for d in range(chips):
            gather_copy(j, d).wait_send()
        for d in range(1, chips):
            forward_copy(j, d).wait_send()
        return 0

    lax.fori_loop(0, 6, drain, 0)


def solution(mesh):
    n_lat, n_lon = mesh.shape["lat"], mesh.shape["lon"]

    def per_device(*args):
        rows = args[0].shape[1]
        total = n_lat * rows
        ext = rows + 2 * TOP
        blocks = (rows + 2 * HALO) // BLOCK
        tiles = -(-len(FIELDS) * blocks // 16)
        chips = n_lat // 2
        vmem = lambda *shape: pltpu.VMEM(shape, jnp.float32)
        dma = lambda *shape: pltpu.SemaphoreType.DMA(shape)
        out = jax.ShapeDtypeStruct((12, rows, 128), jnp.float32)
        return tuple(pl.pallas_call(
            functools.partial(kernel, n_lat, n_lon, rows),
            out_shape=[out] * 3,
            in_specs=[pl.BlockSpec(memory_space=pl.ANY)] * 9,
            out_specs=[pl.BlockSpec(memory_space=pl.ANY)] * 3,
            scratch_shapes=[
                vmem(12, rows, 128), vmem(12, rows, 128), pltpu.VMEM((rows, 128), jnp.int32), vmem(128, 128),
                vmem(ext, total), vmem(39, ext, 128), vmem(39, ext, 128), vmem(24, ext, 128), vmem(24, ext, 128),
                vmem(24, ext, 128), vmem(24, ext, 128), vmem(24, ext, 128), vmem(24, ext, 128),
                vmem(8, ext, 128), vmem(6, total, 256), vmem(2, ext, 128),
                vmem(tiles, BLOCK, 128), vmem(tiles, BLOCK, 128), vmem(tiles, BLOCK, 128),
                vmem(6, BLOCK, 128), vmem(6, BLOCK, 128), vmem(6, BLOCK, 128), vmem(12, rows, 128),
                dma(9), dma(6, chips), dma(6, chips), dma(6, chips - 1), dma(6, chips - 1),
                dma(4), dma(4), dma(2), dma(2), dma(6, 2), dma(6, 2), dma(6, 6),
            ],
            compiler_params=pltpu.CompilerParams(
                collective_id=0, has_side_effects=True, vmem_limit_bytes=50 * 1024 * 1024),
            cost_estimate=pl.CostEstimate(flops=1_000_000_000, bytes_accessed=6_000_000, transcendentals=0),
        )(*args))

    placed = (P(None, "lat", "lon"),) * 4 + (P("lat", "lon"),) * 3 + (P("lon", None), P("lat", "lon"))
    return jax.shard_map(
        per_device, mesh=mesh, in_specs=placed, out_specs=(P(None, "lat", "lon"),) * 3, check_vma=False)
```

```python
import functools
import math

import jax
import jax.numpy as jnp
from jax import lax
from jax.experimental import pallas as pl
from jax.experimental.pallas import tpu as pltpu
from jax.sharding import PartitionSpec as P

FREQS = [1.9323, 2.0, 1.896, 2.0055, 1.0027, 0.9295]
MESH = pl.DeviceIdType.MESH
HIGH = lax.Precision.HIGHEST
TOP = 16
HALO = 8
SENT = 4
BLOCK = 16
STATICS = (36, 37, 38)
FIELDS = tuple(range(24)) + STATICS


def freq_of(j):
    w = jnp.float32(FREQS[0])
    for i in range(1, 6):
        w = jnp.where(j == i, jnp.float32(FREQS[i]), w)
    return w


def kernel(
    n_lat, n_lon, rows,
    elev_h, equil_h, u_h, v_h, dep_h, drag_h, mask_h, lon_h, lat_h,
    oe_h, ou_h, ov_h,
    elev_v, equil_v, mask_v, lon_v, lg, f, fs, mid, mids, two, twos, co, cos, tt, g,
    geo, x0, zl0, zr0, xp, zlp, zrp, eo,
    load_sem, g_send, g_recv, f_send, f_recv, a_send, a_recv, b_send, b_recv, p_send, p_recv, o_sem,
):
    total = n_lat * rows
    end = TOP + rows
    lo, hi = TOP - HALO, end + HALO
    blocks = (hi - lo) // BLOCK
    lat = lax.axis_index("lat")
    lon = lax.axis_index("lon")
    core, chip = lax.rem(lat, 2), lat // 2
    chips = n_lat // 2
    sib = lat + 1 - 2 * core
    right, left = lax.rem(lon + 1, n_lon), lax.rem(lon + n_lon - 1, n_lon)

    loads = [
        (elev_h, elev_v), (mask_h, mask_v), (equil_h, equil_v),
        (u_h, f.at[0:12, TOP:end]), (v_h, f.at[12:24, TOP:end]),
        (dep_h, f.at[36, TOP:end]), (drag_h, f.at[37, TOP:end]),
        (lat_h, lg.at[TOP:end]), (lon_h, lon_v),
    ]
    loads = [pltpu.make_async_copy(s, d, load_sem.at[i]) for i, (s, d) in enumerate(loads)]
    for c in loads:
        c.start()

    barrier = pltpu.get_barrier_semaphore()
    for d in range(1, n_lat):
        pl.semaphore_signal(barrier, inc=1, device_id={"lat": lax.rem(lat + d, n_lat)}, device_id_type=MESH)
    for side in (left, right):
        pl.semaphore_signal(barrier, inc=1, device_id={"lon": side}, device_id_type=MESH)

    own = pl.ds(pl.multiple_of(lat * rows, 8), rows)
    loads[0].wait()
    loads[1].wait()
    f[38, TOP:end] = mask_v[...].astype(jnp.float32)

    def make_source(j, _):
        wet = f[38, TOP:end]
        g[j, own, 0:128] = wet * elev_v[j]
        g[j, own, 128:256] = wet * elev_v[j + 6]
        return 0

    lax.fori_loop(0, 6, make_source, 0)
    for c in loads[2:]:
        c.wait()

    def make_gap(k, _):
        f[24 + k, TOP:end] = elev_v[k] - equil_v[k]
        return 0

    lax.fori_loop(0, 12, make_gap, 0)

    pl.semaphore_wait(barrier, n_lat + 1)

    def remote(src, dst, ss, rs, where):
        return pltpu.make_async_remote_copy(
            src_ref=src, dst_ref=dst, send_sem=ss, recv_sem=rs, device_id=where, device_id_type=MESH)

    def block_of(d):
        return pl.ds(pl.multiple_of((lax.rem(chip + chips - d, chips) * 2 + core) * rows, 8), rows)

    def gather_copy(j, d):
        where = sib if d == 0 else lax.rem(chip + d, chips) * 2 + core
        return remote(g.at[j, own], g.at[j, own], g_send.at[j, d], g_recv.at[j, d], {"lat": where})

    def forward_copy(j, d):
        rows_d = block_of(d)
        return remote(g.at[j, rows_d], g.at[j, rows_d], f_send.at[j, d - 1], f_recv.at[j, d - 1], {"lat": sib})

    def start_gather(j, _):
        for d in range(1, chips):
            gather_copy(j, d).start()
        gather_copy(j, 0).start()
        return 0

    up = [remote(f.at[:, TOP:TOP + SENT], f.at[:, end:end + SENT], a_send.at[0], a_recv.at[0], {"lat": lax.max(lat - 1, 0)}),
          remote(lg.at[TOP:TOP + SENT], lg.at[end:end + SENT], a_send.at[1], a_recv.at[1], {"lat": lax.max(lat - 1, 0)})]
    down = [remote(f.at[:, end - SENT:end], f.at[:, TOP - SENT:TOP], a_send.at[2], a_recv.at[2], {"lat": lax.min(lat + 1, n_lat - 1)}),
            remote(lg.at[end - SENT:end], lg.at[TOP - SENT:TOP], a_send.at[3], a_recv.at[3], {"lat": lax.min(lat + 1, n_lat - 1)})]

    @pl.when(lat > 0)
    def _():
        for c in up:
            c.start()

    @pl.when(lat < n_lat - 1)
    def _():
        for c in down:
            c.start()

    lax.fori_loop(0, 6, start_gather, 0)

    @pl.when(lat == 0)
    def _():
        f[:, lo:TOP] = jnp.zeros((39, HALO, 128), jnp.float32)
        lg[lo:TOP] = jnp.zeros((HALO, total), jnp.float32)

    @pl.when(lat == n_lat - 1)
    def _():
        f[:, end:hi] = jnp.zeros((39, HALO, 128), jnp.float32)
        lg[end:hi] = jnp.zeros((HALO, total), jnp.float32)

    row = lax.broadcasted_iota(jnp.int32, (hi + HALO, 128), 0) + (lat * rows - TOP)
    angle = (-80.0 + 160.0 * (row.astype(jnp.float32) + 0.5) / total) * (math.pi / 180.0)
    geo[0] = 1.0 / jnp.cos(angle)
    geo[1] = 2.0 * jnp.sin(angle)

    @pl.when(lat > 0)
    def _():
        for c in up:
            c.wait_send()
        for c in down:
            c.wait_recv()

    @pl.when(lat < n_lat - 1)
    def _():
        for c in down:
            c.wait_send()
        for c in up:
            c.wait_recv()

    lane = lax.broadcasted_iota(jnp.int32, (BLOCK, 128), 1)
    shifted = lax.rem(lane + 124, 128)
    window = shifted // 8
    from_left = lax.rem(shifted, 8) < 4

    def pack(pieces):
        packed = jnp.zeros((BLOCK, 128), jnp.float32)
        for pos, piece in enumerate(pieces):
            shift = (8 * pos + 8) % 128
            rolled = pltpu.roll(piece, shift, 1) if shift else piece
            packed = jnp.where(window == pos, rolled, packed)
        return packed

    def unpack(z, pos):
        shift = (128 - (8 * pos + 8)) % 128
        return pltpu.roll(z, shift, 1) if shift else z

    slots = [(fi, b) for fi in FIELDS for b in range(blocks)]
    tiles = -(-len(slots) // 16)
    for t in range(tiles):
        part = slots[16 * t:16 * t + 16]
        x0[t] = pack([f[fi, lo + BLOCK * b:lo + BLOCK * b + BLOCK] for fi, b in part])
    edge = [remote(x0, zl0, b_send.at[0], b_recv.at[0], {"lon": right}),
            remote(x0, zr0, b_send.at[1], b_recv.at[1], {"lon": left})]
    for c in edge:
        c.start()

    def coefficients(fields, coefs, j):
        w = freq_of(j)
        for b in range(blocks):
            rs = slice(lo + BLOCK * b, lo + BLOCK * b + BLOCK)
            d = fields[37, rs] + 2.0
            c = geo[1, rs]
            det_r = d * d - w * w + c * c
            det_i = 2.0 * d * w
            inv = fields[38, rs] * 0.5 / (det_r * det_r + det_i * det_i)
            coefs[4 * j, rs] = (d * det_r + w * det_i) * inv
            coefs[4 * j + 1, rs] = (w * det_r - d * det_i) * inv
            coefs[4 * j + 2, rs] = c * det_r * inv
            coefs[4 * j + 3, rs] = -c * det_i * inv

    def coef_main(j, _):
        coefficients(f, co, j)
        return 0

    def coef_side(j, _):
        coefficients(fs, cos, j)
        return 0

    lax.fori_loop(0, 6, coef_main, 0)
    first_lane, last_lane = lane == 0, lane == 127

    def strips(j):
        return [remote(xp.at[j], zlp.at[j], p_send.at[j, 0], p_recv.at[j, 0], {"lon": right}),
                remote(xp.at[j], zrp.at[j], p_send.at[j, 1], p_recv.at[j, 1], {"lon": left})]

    def outs(j):
        copies = []
        for part in range(2):
            k = j + 6 * part
            copies += [
                pltpu.make_async_copy(eo.at[k], oe_h.at[k], o_sem.at[j, 3 * part]),
                pltpu.make_async_copy(two.at[k, TOP:end], ou_h.at[k], o_sem.at[j, 3 * part + 1]),
                pltpu.make_async_copy(two.at[12 + k, TOP:end], ov_h.at[k], o_sem.at[j, 3 * part + 2]),
            ]
        return copies

    def passing(j):
        for d in range(1, chips):
            gather_copy(j, d).wait_recv()
            forward_copy(j, d).start()

    def loading(j):
        gather_copy(j, 0).wait_recv()
        for d in range(1, chips):
            forward_copy(j, d).wait_recv()
        both = jnp.dot(lg[lo:hi], g[j], precision=HIGH, preferred_element_type=jnp.float32)
        for part in range(2):
            k = 24 + j + 6 * part
            sal = lax.dot_general(
                both[:, 128 * part:128 * part + 128], lon_v[...], (((1,), (1,)), ((), ())),
                precision=HIGH, preferred_element_type=jnp.float32)
            f[k, lo:hi] = f[k, lo:hi] - sal
        xp[j] = pack([
            f[24 + j + 6 * part, lo + BLOCK * b:lo + BLOCK * b + BLOCK]
            for part in range(2) for b in range(blocks)])
        for c in strips(j):
            c.start()

    def east_west(m, s):
        em, es = pltpu.roll(m, 127, 1), pltpu.roll(s, 127, 1)
        wm, ws = pltpu.roll(m, 1, 1), pltpu.roll(s, 1, 1)
        return (jnp.where(last_lane, es, em), jnp.where(last_lane, em, es),
                jnp.where(first_lane, ws, wm), jnp.where(first_lane, wm, ws))

    def relax(src, srcs, dst, dsts, j, b, side_v):
        r0 = lo + BLOCK * b
        rs, rn, ro = slice(r0, r0 + BLOCK), slice(r0 + 1, r0 + 1 + BLOCK), slice(r0 - 1, r0 - 1 + BLOCK)
        pm, ps = [], []
        for i in range(4):
            k = j + 6 * i
            em, es, wm, ws = east_west(src[k, rs], srcs[k, rs])
            pm.append(tt[i, rs] + (em + wm + src[k, rn] + src[k, ro]))
            ps.append(tt[4 + i, rs] + (es + ws + srcs[k, rn] + srcs[k, ro]))
        for push, coefs, to, with_v in ((pm, co, dst, True), (ps, cos, dsts, side_v)):
            ar, ai, br, bi = (coefs[4 * j + i, rs] for i in range(4))
            ur, ui, vr, vi = push
            to[j, rs] = ar * ur - ai * ui + br * vr - bi * vi
            to[j + 6, rs] = ar * ui + ai * ur + br * vi + bi * vr
            if with_v:
                to[j + 12, rs] = ar * vr - ai * vi - br * ur + bi * ui
                to[j + 18, rs] = ar * vi + ai * vr - br * ui - bi * ur

    def finish(j):
        for c in strips(j):
            c.wait()
        z = jnp.where(from_left, zlp[j], zrp[j])
        for part in range(2):
            for b in range(blocks):
                fs[24 + j + 6 * part, lo + BLOCK * b:lo + BLOCK * b + BLOCK] = unpack(z, part * blocks + b)
        for b in range(blocks):
            r0 = lo + BLOCK * b
            rs, rn, ro = slice(r0, r0 + BLOCK), slice(r0 + 1, r0 + 1 + BLOCK), slice(r0 - 1, r0 - 1 + BLOCK)
            stretch = geo[0, rs]
            dm, ds = f[36, rs], fs[36, rs]
            for part in range(2):
                k = 24 + j + 6 * part
                em, es, wm, ws = east_west(f[k, rs], fs[k, rs])
                tt[part, rs] = dm * stretch * (wm - em)
                tt[4 + part, rs] = ds * stretch * (ws - es)
                tt[2 + part, rs] = dm * (f[k, ro] - f[k, rn])
                tt[6 + part, rs] = ds * (fs[k, ro] - fs[k, rn])
        for b in range(blocks):
            relax(f, fs, mid, mids, j, b, True)
        for b in range(blocks):
            relax(mid, mids, two, twos, j, b, False)
        scale = 0.5 / freq_of(j)
        for b in range(rows // BLOCK):
            r0 = TOP + BLOCK * b
            rs, rn, ro = slice(r0, r0 + BLOCK), slice(r0 + 1, r0 + 1 + BLOCK), slice(r0 - 1, r0 - 1 + BLOCK)
            stretch = geo[0, rs]
            wet = f[38, rs] * scale
            spread = []
            for part in range(2):
                k = j + 6 * part
                em, _, wm, _ = east_west(two[k, rs], twos[k, rs])
                spread.append((em - wm) * stretch + (two[12 + k, rn] - two[12 + k, ro]))
            eo[j, BLOCK * b:BLOCK * b + BLOCK] = -wet * spread[1]
            eo[j + 6, BLOCK * b:BLOCK * b + BLOCK] = wet * spread[0]
        for c in outs(j):
            c.start()

    passing(0)
    passing(1)
    loading(0)
    loading(1)
    for c in edge:
        c.wait()
    for t in range(tiles):
        z = jnp.where(from_left, zl0[t], zr0[t])
        for pos, (fi, b) in enumerate(slots[16 * t:16 * t + 16]):
            fs[fi, lo + BLOCK * b:lo + BLOCK * b + BLOCK] = unpack(z, pos)
    lax.fori_loop(0, 6, coef_side, 0)

    def step(j, _):
        @pl.when(j < 6)
        def _():
            passing(lax.min(j, 5))

        @pl.when(jnp.logical_and(j > 2, j < 7))
        def _():
            loading(lax.max(lax.min(j - 1, 5), 0))

        @pl.when(j > 2)
        def _():
            finish(lax.max(j - 3, 0))

        return 0

    lax.fori_loop(2, 9, step, 0)

    def drain(j, _):
        for c in outs(j):
            c.wait()
        for d in range(chips):
            gather_copy(j, d).wait_send()
        for d in range(1, chips):
            forward_copy(j, d).wait_send()
        return 0

    lax.fori_loop(0, 6, drain, 0)


def solution(mesh):
    n_lat, n_lon = mesh.shape["lat"], mesh.shape["lon"]

    def per_device(*args):
        rows = args[0].shape[1]
        total = n_lat * rows
        ext = rows + 2 * TOP
        blocks = (rows + 2 * HALO) // BLOCK
        tiles = -(-len(FIELDS) * blocks // 16)
        chips = n_lat // 2
        vmem = lambda *shape: pltpu.VMEM(shape, jnp.float32)
        dma = lambda *shape: pltpu.SemaphoreType.DMA(shape)
        out = jax.ShapeDtypeStruct((12, rows, 128), jnp.float32)
        return tuple(pl.pallas_call(
            functools.partial(kernel, n_lat, n_lon, rows),
            out_shape=[out] * 3,
            in_specs=[pl.BlockSpec(memory_space=pltpu.HBM)] * 9,
            out_specs=[pl.BlockSpec(memory_space=pltpu.HBM)] * 3,
            scratch_shapes=[
                vmem(12, rows, 128), vmem(12, rows, 128), pltpu.VMEM((rows, 128), jnp.int32), vmem(128, 128),
                vmem(ext, total), vmem(39, ext, 128), vmem(39, ext, 128), vmem(24, ext, 128), vmem(24, ext, 128),
                vmem(24, ext, 128), vmem(24, ext, 128), vmem(24, ext, 128), vmem(24, ext, 128),
                vmem(8, ext, 128), vmem(6, total, 256), vmem(2, ext, 128),
                vmem(tiles, BLOCK, 128), vmem(tiles, BLOCK, 128), vmem(tiles, BLOCK, 128),
                vmem(6, BLOCK, 128), vmem(6, BLOCK, 128), vmem(6, BLOCK, 128), vmem(12, rows, 128),
                dma(9), dma(6, chips), dma(6, chips), dma(6, chips - 1), dma(6, chips - 1),
                dma(4), dma(4), dma(2), dma(2), dma(6, 2), dma(6, 2), dma(6, 6),
            ],
            compiler_params=pltpu.CompilerParams(
                collective_id=0, has_side_effects=True, vmem_limit_bytes=62 * 1024 * 1024),
            cost_estimate=pl.CostEstimate(flops=1_000_000_000, bytes_accessed=6_000_000, transcendentals=0),
        )(*args))

    placed = (P(None, "lat", "lon"),) * 4 + (P("lat", "lon"),) * 3 + (P("lon", None), P("lat", "lon"))
    return jax.shard_map(
        per_device, mesh=mesh, in_specs=placed, out_specs=(P(None, "lat", "lon"),) * 3, check_vma=False)
```

```python
import functools
import math

import jax
import jax.numpy as jnp
from jax import lax
from jax.experimental import pallas as pl
from jax.experimental.pallas import tpu as pltpu
from jax.sharding import PartitionSpec as P

FREQS = [1.9323, 2.0, 1.896, 2.0055, 1.0027, 0.9295]
MESH = pl.DeviceIdType.MESH
HIGH = lax.Precision.HIGHEST
TOP = 16
HALO = 8
SENT = 4
BLOCK = 16
STATICS = (36, 37, 38)
FIELDS = tuple(range(24)) + STATICS


def freq_of(j):
    w = jnp.float32(FREQS[0])
    for i in range(1, 6):
        w = jnp.where(j == i, jnp.float32(FREQS[i]), w)
    return w


def kernel(
    n_lat, n_lon, rows,
    elev_h, equil_h, u_h, v_h, dep_h, drag_h, mask_h, lon_h, lat_h,
    oe_h, ou_h, ov_h,
    elev_v, equil_v, mask_v, lon_v, lg, f, fs, mid, mids, two, twos, co, cos, tt, g,
    geo, x0, zl0, zr0, xp, zlp, zrp, eo,
    load_sem, g_send, g_recv, f_send, f_recv, a_send, a_recv, b_send, b_recv, p_send, p_recv, o_sem,
):
    total = n_lat * rows
    end = TOP + rows
    lo, hi = TOP - HALO, end + HALO
    blocks = (hi - lo) // BLOCK
    lat = lax.axis_index("lat")
    lon = lax.axis_index("lon")
    core, chip = lax.rem(lat, 2), lat // 2
    chips = n_lat // 2
    sib = lat + 1 - 2 * core
    right, left = lax.rem(lon + 1, n_lon), lax.rem(lon + n_lon - 1, n_lon)

    loads = [
        (elev_h, elev_v), (mask_h, mask_v), (equil_h, equil_v),
        (u_h, f.at[0:12, TOP:end]), (v_h, f.at[12:24, TOP:end]),
        (dep_h, f.at[36, TOP:end]), (drag_h, f.at[37, TOP:end]),
        (lat_h, lg.at[TOP:end]), (lon_h, lon_v),
    ]
    loads = [pltpu.make_async_copy(s, d, load_sem.at[i]) for i, (s, d) in enumerate(loads)]
    for c in loads:
        c.start()

    barrier = pltpu.get_barrier_semaphore()
    for d in range(1, n_lat):
        pl.semaphore_signal(barrier, inc=1, device_id={"lat": lax.rem(lat + d, n_lat)}, device_id_type=MESH)
    for side in (left, right):
        pl.semaphore_signal(barrier, inc=1, device_id={"lon": side}, device_id_type=MESH)

    own = pl.ds(pl.multiple_of(lat * rows, 8), rows)
    loads[0].wait()
    loads[1].wait()
    f[38, TOP:end] = mask_v[...].astype(jnp.float32)

    def make_source(j, _):
        wet = f[38, TOP:end]
        g[j, own, 0:128] = wet * elev_v[j]
        g[j, own, 128:256] = wet * elev_v[j + 6]
        return 0

    lax.fori_loop(0, 6, make_source, 0)
    for c in loads[2:]:
        c.wait()

    def make_gap(k, _):
        f[24 + k, TOP:end] = elev_v[k] - equil_v[k]
        return 0

    lax.fori_loop(0, 12, make_gap, 0)

    pl.semaphore_wait(barrier, n_lat + 1)

    def remote(src, dst, ss, rs, where):
        return pltpu.make_async_remote_copy(
            src_ref=src, dst_ref=dst, send_sem=ss, recv_sem=rs, device_id=where, device_id_type=MESH)

    def block_of(d):
        return pl.ds(pl.multiple_of((lax.rem(chip + chips - d, chips) * 2 + core) * rows, 8), rows)

    def gather_copy(j, d):
        where = sib if d == 0 else lax.rem(chip + d, chips) * 2 + core
        return remote(g.at[j, own], g.at[j, own], g_send.at[j, d], g_recv.at[j, d], {"lat": where})

    def forward_copy(j, d):
        rows_d = block_of(d)
        return remote(g.at[j, rows_d], g.at[j, rows_d], f_send.at[j, d - 1], f_recv.at[j, d - 1], {"lat": sib})

    def start_gather(j, _):
        for d in range(1, chips):
            gather_copy(j, d).start()
        gather_copy(j, 0).start()
        return 0

    up = [remote(f.at[:, TOP:TOP + SENT], f.at[:, end:end + SENT], a_send.at[0], a_recv.at[0], {"lat": lax.max(lat - 1, 0)}),
          remote(lg.at[TOP:TOP + SENT], lg.at[end:end + SENT], a_send.at[1], a_recv.at[1], {"lat": lax.max(lat - 1, 0)})]
    down = [remote(f.at[:, end - SENT:end], f.at[:, TOP - SENT:TOP], a_send.at[2], a_recv.at[2], {"lat": lax.min(lat + 1, n_lat - 1)}),
            remote(lg.at[end - SENT:end], lg.at[TOP - SENT:TOP], a_send.at[3], a_recv.at[3], {"lat": lax.min(lat + 1, n_lat - 1)})]

    @pl.when(lat > 0)
    def _():
        for c in up:
            c.start()

    @pl.when(lat < n_lat - 1)
    def _():
        for c in down:
            c.start()

    lax.fori_loop(0, 6, start_gather, 0)

    @pl.when(lat == 0)
    def _():
        f[:, lo:TOP] = jnp.zeros((39, HALO, 128), jnp.float32)
        lg[lo:TOP] = jnp.zeros((HALO, total), jnp.float32)

    @pl.when(lat == n_lat - 1)
    def _():
        f[:, end:hi] = jnp.zeros((39, HALO, 128), jnp.float32)
        lg[end:hi] = jnp.zeros((HALO, total), jnp.float32)

    row = lax.broadcasted_iota(jnp.int32, (hi + HALO, 128), 0) + (lat * rows - TOP)
    angle = (-80.0 + 160.0 * (row.astype(jnp.float32) + 0.5) / total) * (math.pi / 180.0)
    geo[0] = 1.0 / jnp.cos(angle)
    geo[1] = 2.0 * jnp.sin(angle)

    @pl.when(lat > 0)
    def _():
        for c in up:
            c.wait_send()
        for c in down:
            c.wait_recv()

    @pl.when(lat < n_lat - 1)
    def _():
        for c in down:
            c.wait_send()
        for c in up:
            c.wait_recv()

    lane = lax.broadcasted_iota(jnp.int32, (BLOCK, 128), 1)
    shifted = lax.rem(lane + 124, 128)
    window = shifted // 8
    from_left = lax.rem(shifted, 8) < 4

    def pack(pieces):
        packed = jnp.zeros((BLOCK, 128), jnp.float32)
        for pos, piece in enumerate(pieces):
            shift = (8 * pos + 8) % 128
            rolled = pltpu.roll(piece, shift, 1) if shift else piece
            packed = jnp.where(window == pos, rolled, packed)
        return packed

    def unpack(z, pos):
        shift = (128 - (8 * pos + 8)) % 128
        return pltpu.roll(z, shift, 1) if shift else z

    slots = [(fi, b) for fi in FIELDS for b in range(blocks)]
    tiles = -(-len(slots) // 16)
    for t in range(tiles):
        part = slots[16 * t:16 * t + 16]
        x0[t] = pack([f[fi, lo + BLOCK * b:lo + BLOCK * b + BLOCK] for fi, b in part])
    edge = [remote(x0, zl0, b_send.at[0], b_recv.at[0], {"lon": right}),
            remote(x0, zr0, b_send.at[1], b_recv.at[1], {"lon": left})]
    for c in edge:
        c.start()

    def coefficients(fields, coefs, j):
        w = freq_of(j)
        for b in range(blocks):
            rs = slice(lo + BLOCK * b, lo + BLOCK * b + BLOCK)
            d = fields[37, rs] + 2.0
            c = geo[1, rs]
            det_r = d * d - w * w + c * c
            det_i = 2.0 * d * w
            inv = fields[38, rs] * 0.5 / (det_r * det_r + det_i * det_i)
            coefs[4 * j, rs] = (d * det_r + w * det_i) * inv
            coefs[4 * j + 1, rs] = (w * det_r - d * det_i) * inv
            coefs[4 * j + 2, rs] = c * det_r * inv
            coefs[4 * j + 3, rs] = -c * det_i * inv

    def coef_main(j, _):
        coefficients(f, co, j)
        return 0

    def coef_side(j, _):
        coefficients(fs, cos, j)
        return 0

    lax.fori_loop(0, 6, coef_main, 0)
    first_lane, last_lane = lane == 0, lane == 127

    def strips(j):
        return [remote(xp.at[j], zlp.at[j], p_send.at[j, 0], p_recv.at[j, 0], {"lon": right}),
                remote(xp.at[j], zrp.at[j], p_send.at[j, 1], p_recv.at[j, 1], {"lon": left})]

    def outs(j):
        copies = []
        for part in range(2):
            k = j + 6 * part
            copies += [
                pltpu.make_async_copy(eo.at[k], oe_h.at[k], o_sem.at[j, 3 * part]),
                pltpu.make_async_copy(two.at[k, TOP:end], ou_h.at[k], o_sem.at[j, 3 * part + 1]),
                pltpu.make_async_copy(two.at[12 + k, TOP:end], ov_h.at[k], o_sem.at[j, 3 * part + 2]),
            ]
        return copies

    def passing(j):
        for d in range(1, chips):
            gather_copy(j, d).wait_recv()
            forward_copy(j, d).start()

    def loading(j):
        gather_copy(j, 0).wait_recv()
        for d in range(1, chips):
            forward_copy(j, d).wait_recv()
        both = jnp.dot(lg[lo:hi], g[j], precision=HIGH, preferred_element_type=jnp.float32)
        for part in range(2):
            k = 24 + j + 6 * part
            sal = lax.dot_general(
                both[:, 128 * part:128 * part + 128], lon_v[...], (((1,), (1,)), ((), ())),
                precision=HIGH, preferred_element_type=jnp.float32)
            f[k, lo:hi] = f[k, lo:hi] - sal
        xp[j] = pack([
            f[24 + j + 6 * part, lo + BLOCK * b:lo + BLOCK * b + BLOCK]
            for part in range(2) for b in range(blocks)])
        for c in strips(j):
            c.start()

    def east_west(m, s):
        em, es = pltpu.roll(m, 127, 1), pltpu.roll(s, 127, 1)
        wm, ws = pltpu.roll(m, 1, 1), pltpu.roll(s, 1, 1)
        return (jnp.where(last_lane, es, em), jnp.where(last_lane, em, es),
                jnp.where(first_lane, ws, wm), jnp.where(first_lane, wm, ws))

    def relax(src, srcs, dst, dsts, j, b, side_v):
        r0 = lo + BLOCK * b
        rs, rn, ro = slice(r0, r0 + BLOCK), slice(r0 + 1, r0 + 1 + BLOCK), slice(r0 - 1, r0 - 1 + BLOCK)
        pm, ps = [], []
        for i in range(4):
            k = j + 6 * i
            em, es, wm, ws = east_west(src[k, rs], srcs[k, rs])
            pm.append(tt[i, rs] + (em + wm + src[k, rn] + src[k, ro]))
            ps.append(tt[4 + i, rs] + (es + ws + srcs[k, rn] + srcs[k, ro]))
        for push, coefs, to, with_v in ((pm, co, dst, True), (ps, cos, dsts, side_v)):
            ar, ai, br, bi = (coefs[4 * j + i, rs] for i in range(4))
            ur, ui, vr, vi = push
            to[j, rs] = ar * ur - ai * ui + br * vr - bi * vi
            to[j + 6, rs] = ar * ui + ai * ur + br * vi + bi * vr
            if with_v:
                to[j + 12, rs] = ar * vr - ai * vi - br * ur + bi * ui
                to[j + 18, rs] = ar * vi + ai * vr - br * ui - bi * ur

    def finish(j):
        for c in strips(j):
            c.wait()
        z = jnp.where(from_left, zlp[j], zrp[j])
        for part in range(2):
            for b in range(blocks):
                fs[24 + j + 6 * part, lo + BLOCK * b:lo + BLOCK * b + BLOCK] = unpack(z, part * blocks + b)
        for b in range(blocks):
            r0 = lo + BLOCK * b
            rs, rn, ro = slice(r0, r0 + BLOCK), slice(r0 + 1, r0 + 1 + BLOCK), slice(r0 - 1, r0 - 1 + BLOCK)
            stretch = geo[0, rs]
            dm, ds = f[36, rs], fs[36, rs]
            for part in range(2):
                k = 24 + j + 6 * part
                em, es, wm, ws = east_west(f[k, rs], fs[k, rs])
                tt[part, rs] = dm * stretch * (wm - em)
                tt[4 + part, rs] = ds * stretch * (ws - es)
                tt[2 + part, rs] = dm * (f[k, ro] - f[k, rn])
                tt[6 + part, rs] = ds * (fs[k, ro] - fs[k, rn])
        for b in range(blocks):
            relax(f, fs, mid, mids, j, b, True)
        for b in range(blocks):
            relax(mid, mids, two, twos, j, b, False)
        scale = 0.5 / freq_of(j)
        for b in range(rows // BLOCK):
            r0 = TOP + BLOCK * b
            rs, rn, ro = slice(r0, r0 + BLOCK), slice(r0 + 1, r0 + 1 + BLOCK), slice(r0 - 1, r0 - 1 + BLOCK)
            stretch = geo[0, rs]
            wet = f[38, rs] * scale
            spread = []
            for part in range(2):
                k = j + 6 * part
                em, _, wm, _ = east_west(two[k, rs], twos[k, rs])
                spread.append((em - wm) * stretch + (two[12 + k, rn] - two[12 + k, ro]))
            eo[j, BLOCK * b:BLOCK * b + BLOCK] = -wet * spread[1]
            eo[j + 6, BLOCK * b:BLOCK * b + BLOCK] = wet * spread[0]
        for c in outs(j):
            c.start()

    passing(0)
    passing(1)
    loading(0)
    loading(1)
    for c in edge:
        c.wait()
    for t in range(tiles):
        z = jnp.where(from_left, zl0[t], zr0[t])
        for pos, (fi, b) in enumerate(slots[16 * t:16 * t + 16]):
            fs[fi, lo + BLOCK * b:lo + BLOCK * b + BLOCK] = unpack(z, pos)
    lax.fori_loop(0, 6, coef_side, 0)

    def step(j, _):
        @pl.when(j < 6)
        def _():
            passing(lax.min(j, 5))

        @pl.when(jnp.logical_and(j > 2, j < 7))
        def _():
            loading(lax.max(lax.min(j - 1, 5), 0))

        @pl.when(j > 2)
        def _():
            finish(lax.max(j - 3, 0))

        return 0

    lax.fori_loop(2, 9, step, 0)

    def drain(j, _):
        for c in outs(j):
            c.wait()
        for d in range(chips):
            gather_copy(j, d).wait_send()
        for d in range(1, chips):
            forward_copy(j, d).wait_send()
        return 0

    lax.fori_loop(0, 6, drain, 0)


def solution(mesh):
    n_lat, n_lon = mesh.shape["lat"], mesh.shape["lon"]

    def per_device(*args):
        rows = args[0].shape[1]
        total = n_lat * rows
        ext = rows + 2 * TOP
        blocks = (rows + 2 * HALO) // BLOCK
        tiles = -(-len(FIELDS) * blocks // 16)
        chips = n_lat // 2
        vmem = lambda *shape: pltpu.VMEM(shape, jnp.float32)
        dma = lambda *shape: pltpu.SemaphoreType.DMA(shape)
        out = jax.ShapeDtypeStruct((12, rows, 128), jnp.float32)
        args = [pltpu.with_memory_space_constraint(a, pltpu.HBM) for a in args]
        return tuple(pl.pallas_call(
            functools.partial(kernel, n_lat, n_lon, rows),
            out_shape=[out] * 3,
            in_specs=[pl.BlockSpec(memory_space=pltpu.HBM)] * 9,
            out_specs=[pl.BlockSpec(memory_space=pl.ANY)] * 3,
            scratch_shapes=[
                vmem(12, rows, 128), vmem(12, rows, 128), pltpu.VMEM((rows, 128), jnp.int32), vmem(128, 128),
                vmem(ext, total), vmem(39, ext, 128), vmem(39, ext, 128), vmem(24, ext, 128), vmem(24, ext, 128),
                vmem(24, ext, 128), vmem(24, ext, 128), vmem(24, ext, 128), vmem(24, ext, 128),
                vmem(8, ext, 128), vmem(6, total, 256), vmem(2, ext, 128),
                vmem(tiles, BLOCK, 128), vmem(tiles, BLOCK, 128), vmem(tiles, BLOCK, 128),
                vmem(6, BLOCK, 128), vmem(6, BLOCK, 128), vmem(6, BLOCK, 128), vmem(12, rows, 128),
                dma(9), dma(6, chips), dma(6, chips), dma(6, chips - 1), dma(6, chips - 1),
                dma(4), dma(4), dma(2), dma(2), dma(6, 2), dma(6, 2), dma(6, 6),
            ],
            compiler_params=pltpu.CompilerParams(
                collective_id=0, has_side_effects=True, vmem_limit_bytes=48 * 1024 * 1024),
            cost_estimate=pl.CostEstimate(flops=1_000_000_000, bytes_accessed=6_000_000, transcendentals=0),
        )(*args))

    placed = (P(None, "lat", "lon"),) * 4 + (P("lat", "lon"),) * 3 + (P("lon", None), P("lat", "lon"))
    return jax.shard_map(
        per_device, mesh=mesh, in_specs=placed, out_specs=(P(None, "lat", "lon"),) * 3, check_vma=False)
```

```python
import functools
import math

import jax
import jax.numpy as jnp
from jax import lax
from jax.experimental import pallas as pl
from jax.experimental.pallas import tpu as pltpu
from jax.sharding import PartitionSpec as P

FREQS = [1.9323, 2.0, 1.896, 2.0055, 1.0027, 0.9295]
MESH = pl.DeviceIdType.MESH
HIGH = lax.Precision.HIGHEST
TOP = 16
HALO = 8
SENT = 4
BLOCK = 16
STATICS = (36, 37, 38)
FIELDS = tuple(range(24)) + STATICS


def freq_of(j):
    w = jnp.float32(FREQS[0])
    for i in range(1, 6):
        w = jnp.where(j == i, jnp.float32(FREQS[i]), w)
    return w


def kernel(
    n_lat, n_lon, rows,
    elev_h, equil_h, u_h, v_h, dep_h, drag_h, mask_h, lon_h, lat_h,
    oe_h, ou_h, ov_h,
    elev_v, equil_v, mask_v, lon_v, lg, f, fs, mid, mids, two, twos, co, cos, tt, g,
    geo, x0, zl0, zr0, xp, zlp, zrp, eo,
    load_sem, g_send, g_recv, f_send, f_recv, a_send, a_recv, b_send, b_recv, p_send, p_recv, o_sem,
):
    total = n_lat * rows
    end = TOP + rows
    lo, hi = TOP - HALO, end + HALO
    blocks = (hi - lo) // BLOCK
    lat = lax.axis_index("lat")
    lon = lax.axis_index("lon")
    core, chip = lax.rem(lat, 2), lat // 2
    chips = n_lat // 2
    sib = lat + 1 - 2 * core
    right, left = lax.rem(lon + 1, n_lon), lax.rem(lon + n_lon - 1, n_lon)

    loads = [
        (elev_h, elev_v), (mask_h, mask_v), (equil_h, equil_v),
        (u_h, f.at[0:12, TOP:end]), (v_h, f.at[12:24, TOP:end]),
        (dep_h, f.at[36, TOP:end]), (drag_h, f.at[37, TOP:end]),
        (lat_h, lg.at[TOP:end]), (lon_h, lon_v),
    ]
    loads = [pltpu.make_async_copy(s, d, load_sem.at[i]) for i, (s, d) in enumerate(loads)]
    for c in loads:
        c.start()

    barrier = pltpu.get_barrier_semaphore()
    for d in range(1, n_lat):
        pl.semaphore_signal(barrier, inc=1, device_id={"lat": lax.rem(lat + d, n_lat)}, device_id_type=MESH)
    for side in (left, right):
        pl.semaphore_signal(barrier, inc=1, device_id={"lon": side}, device_id_type=MESH)

    own = pl.ds(pl.multiple_of(lat * rows, 8), rows)
    loads[0].wait()
    loads[1].wait()
    f[38, TOP:end] = mask_v[...].astype(jnp.float32)

    def make_source(j, _):
        wet = f[38, TOP:end]
        g[j, own, 0:128] = wet * elev_v[j]
        g[j, own, 128:256] = wet * elev_v[j + 6]
        return 0

    lax.fori_loop(0, 6, make_source, 0)
    for c in loads[2:]:
        c.wait()

    def make_gap(k, _):
        f[24 + k, TOP:end] = elev_v[k] - equil_v[k]
        return 0

    lax.fori_loop(0, 12, make_gap, 0)

    pl.semaphore_wait(barrier, n_lat + 1)

    def remote(src, dst, ss, rs, where):
        return pltpu.make_async_remote_copy(
            src_ref=src, dst_ref=dst, send_sem=ss, recv_sem=rs, device_id=where, device_id_type=MESH)

    def block_of(d):
        return pl.ds(pl.multiple_of((lax.rem(chip + chips - d, chips) * 2 + core) * rows, 8), rows)

    def gather_copy(j, d):
        where = sib if d == 0 else lax.rem(chip + d, chips) * 2 + core
        return remote(g.at[j, own], g.at[j, own], g_send.at[j, d], g_recv.at[j, d], {"lat": where})

    def forward_copy(j, d):
        rows_d = block_of(d)
        return remote(g.at[j, rows_d], g.at[j, rows_d], f_send.at[j, d - 1], f_recv.at[j, d - 1], {"lat": sib})

    def start_gather(j, _):
        for d in range(1, chips):
            gather_copy(j, d).start()
        gather_copy(j, 0).start()
        return 0

    up = [remote(f.at[:, TOP:TOP + SENT], f.at[:, end:end + SENT], a_send.at[0], a_recv.at[0], {"lat": lax.max(lat - 1, 0)}),
          remote(lg.at[TOP:TOP + SENT], lg.at[end:end + SENT], a_send.at[1], a_recv.at[1], {"lat": lax.max(lat - 1, 0)})]
    down = [remote(f.at[:, end - SENT:end], f.at[:, TOP - SENT:TOP], a_send.at[2], a_recv.at[2], {"lat": lax.min(lat + 1, n_lat - 1)}),
            remote(lg.at[end - SENT:end], lg.at[TOP - SENT:TOP], a_send.at[3], a_recv.at[3], {"lat": lax.min(lat + 1, n_lat - 1)})]

    @pl.when(lat > 0)
    def _():
        for c in up:
            c.start()

    @pl.when(lat < n_lat - 1)
    def _():
        for c in down:
            c.start()

    lax.fori_loop(0, 6, start_gather, 0)

    @pl.when(lat == 0)
    def _():
        f[:, lo:TOP] = jnp.zeros((39, HALO, 128), jnp.float32)
        lg[lo:TOP] = jnp.zeros((HALO, total), jnp.float32)

    @pl.when(lat == n_lat - 1)
    def _():
        f[:, end:hi] = jnp.zeros((39, HALO, 128), jnp.float32)
        lg[end:hi] = jnp.zeros((HALO, total), jnp.float32)

    row = lax.broadcasted_iota(jnp.int32, (hi + HALO, 128), 0) + (lat * rows - TOP)
    angle = (-80.0 + 160.0 * (row.astype(jnp.float32) + 0.5) / total) * (math.pi / 180.0)
    geo[0] = 1.0 / jnp.cos(angle)
    geo[1] = 2.0 * jnp.sin(angle)

    @pl.when(lat > 0)
    def _():
        for c in up:
            c.wait_send()
        for c in down:
            c.wait_recv()

    @pl.when(lat < n_lat - 1)
    def _():
        for c in down:
            c.wait_send()
        for c in up:
            c.wait_recv()

    lane = lax.broadcasted_iota(jnp.int32, (BLOCK, 128), 1)
    shifted = lax.rem(lane + 124, 128)
    window = shifted // 8
    from_left = lax.rem(shifted, 8) < 4

    def pack(pieces):
        packed = jnp.zeros((BLOCK, 128), jnp.float32)
        for pos, piece in enumerate(pieces):
            shift = (8 * pos + 8) % 128
            rolled = pltpu.roll(piece, shift, 1) if shift else piece
            packed = jnp.where(window == pos, rolled, packed)
        return packed

    def unpack(z, pos):
        shift = (128 - (8 * pos + 8)) % 128
        return pltpu.roll(z, shift, 1) if shift else z

    slots = [(fi, b) for fi in FIELDS for b in range(blocks)]
    tiles = -(-len(slots) // 16)
    for t in range(tiles):
        part = slots[16 * t:16 * t + 16]
        x0[t] = pack([f[fi, lo + BLOCK * b:lo + BLOCK * b + BLOCK] for fi, b in part])
    edge = [remote(x0, zl0, b_send.at[0], b_recv.at[0], {"lon": right}),
            remote(x0, zr0, b_send.at[1], b_recv.at[1], {"lon": left})]
    for c in edge:
        c.start()

    def coefficients(fields, coefs, j):
        w = freq_of(j)
        for b in range(blocks):
            rs = slice(lo + BLOCK * b, lo + BLOCK * b + BLOCK)
            d = fields[37, rs] + 2.0
            c = geo[1, rs]
            det_r = d * d - w * w + c * c
            det_i = 2.0 * d * w
            inv = fields[38, rs] * 0.5 / (det_r * det_r + det_i * det_i)
            coefs[4 * j, rs] = (d * det_r + w * det_i) * inv
            coefs[4 * j + 1, rs] = (w * det_r - d * det_i) * inv
            coefs[4 * j + 2, rs] = c * det_r * inv
            coefs[4 * j + 3, rs] = -c * det_i * inv

    def coef_main(j, _):
        coefficients(f, co, j)
        return 0

    def coef_side(j, _):
        coefficients(fs, cos, j)
        return 0

    lax.fori_loop(0, 6, coef_main, 0)
    first_lane, last_lane = lane == 0, lane == 127

    def strips(j):
        return [remote(xp.at[j], zlp.at[j], p_send.at[j, 0], p_recv.at[j, 0], {"lon": right}),
                remote(xp.at[j], zrp.at[j], p_send.at[j, 1], p_recv.at[j, 1], {"lon": left})]

    def outs(j):
        copies = []
        for part in range(2):
            k = j + 6 * part
            copies += [
                pltpu.make_async_copy(eo.at[k], oe_h.at[k], o_sem.at[j, 3 * part]),
                pltpu.make_async_copy(two.at[k, TOP:end], ou_h.at[k], o_sem.at[j, 3 * part + 1]),
                pltpu.make_async_copy(two.at[12 + k, TOP:end], ov_h.at[k], o_sem.at[j, 3 * part + 2]),
            ]
        return copies

    def passing(j):
        for d in range(1, chips):
            gather_copy(j, d).wait_recv()
            forward_copy(j, d).start()

    def loading(j):
        gather_copy(j, 0).wait_recv()
        for d in range(1, chips):
            forward_copy(j, d).wait_recv()
        both = jnp.dot(lg[lo:hi], g[j], precision=HIGH, preferred_element_type=jnp.float32)
        for part in range(2):
            k = 24 + j + 6 * part
            sal = lax.dot_general(
                both[:, 128 * part:128 * part + 128], lon_v[...], (((1,), (1,)), ((), ())),
                precision=HIGH, preferred_element_type=jnp.float32)
            f[k, lo:hi] = f[k, lo:hi] - sal
        xp[j] = pack([
            f[24 + j + 6 * part, lo + BLOCK * b:lo + BLOCK * b + BLOCK]
            for part in range(2) for b in range(blocks)])
        for c in strips(j):
            c.start()

    def east_west(m, s):
        em, es = pltpu.roll(m, 127, 1), pltpu.roll(s, 127, 1)
        wm, ws = pltpu.roll(m, 1, 1), pltpu.roll(s, 1, 1)
        return (jnp.where(last_lane, es, em), jnp.where(last_lane, em, es),
                jnp.where(first_lane, ws, wm), jnp.where(first_lane, wm, ws))

    def relax(src, srcs, dst, dsts, j, b, side_v):
        r0 = lo + BLOCK * b
        rs, rn, ro = slice(r0, r0 + BLOCK), slice(r0 + 1, r0 + 1 + BLOCK), slice(r0 - 1, r0 - 1 + BLOCK)
        pm, ps = [], []
        for i in range(4):
            k = j + 6 * i
            em, es, wm, ws = east_west(src[k, rs], srcs[k, rs])
            pm.append(tt[i, rs] + (em + wm + src[k, rn] + src[k, ro]))
            ps.append(tt[4 + i, rs] + (es + ws + srcs[k, rn] + srcs[k, ro]))
        for push, coefs, to, with_v in ((pm, co, dst, True), (ps, cos, dsts, side_v)):
            ar, ai, br, bi = (coefs[4 * j + i, rs] for i in range(4))
            ur, ui, vr, vi = push
            to[j, rs] = ar * ur - ai * ui + br * vr - bi * vi
            to[j + 6, rs] = ar * ui + ai * ur + br * vi + bi * vr
            if with_v:
                to[j + 12, rs] = ar * vr - ai * vi - br * ur + bi * ui
                to[j + 18, rs] = ar * vi + ai * vr - br * ui - bi * ur

    def finish(j):
        for c in strips(j):
            c.wait()
        z = jnp.where(from_left, zlp[j], zrp[j])
        for part in range(2):
            for b in range(blocks):
                fs[24 + j + 6 * part, lo + BLOCK * b:lo + BLOCK * b + BLOCK] = unpack(z, part * blocks + b)
        for b in range(blocks):
            r0 = lo + BLOCK * b
            rs, rn, ro = slice(r0, r0 + BLOCK), slice(r0 + 1, r0 + 1 + BLOCK), slice(r0 - 1, r0 - 1 + BLOCK)
            stretch = geo[0, rs]
            dm, ds = f[36, rs], fs[36, rs]
            for part in range(2):
                k = 24 + j + 6 * part
                em, es, wm, ws = east_west(f[k, rs], fs[k, rs])
                tt[part, rs] = dm * stretch * (wm - em)
                tt[4 + part, rs] = ds * stretch * (ws - es)
                tt[2 + part, rs] = dm * (f[k, ro] - f[k, rn])
                tt[6 + part, rs] = ds * (fs[k, ro] - fs[k, rn])
        for b in range(blocks):
            relax(f, fs, mid, mids, j, b, True)
        for b in range(blocks):
            relax(mid, mids, two, twos, j, b, False)
        scale = 0.5 / freq_of(j)
        for b in range(rows // BLOCK):
            r0 = TOP + BLOCK * b
            rs, rn, ro = slice(r0, r0 + BLOCK), slice(r0 + 1, r0 + 1 + BLOCK), slice(r0 - 1, r0 - 1 + BLOCK)
            stretch = geo[0, rs]
            wet = f[38, rs] * scale
            spread = []
            for part in range(2):
                k = j + 6 * part
                em, _, wm, _ = east_west(two[k, rs], twos[k, rs])
                spread.append((em - wm) * stretch + (two[12 + k, rn] - two[12 + k, ro]))
            eo[j, BLOCK * b:BLOCK * b + BLOCK] = -wet * spread[1]
            eo[j + 6, BLOCK * b:BLOCK * b + BLOCK] = wet * spread[0]
        for c in outs(j):
            c.start()

    passing(0)
    passing(1)
    loading(0)
    loading(1)
    for c in edge:
        c.wait()
    for t in range(tiles):
        z = jnp.where(from_left, zl0[t], zr0[t])
        for pos, (fi, b) in enumerate(slots[16 * t:16 * t + 16]):
            fs[fi, lo + BLOCK * b:lo + BLOCK * b + BLOCK] = unpack(z, pos)
    lax.fori_loop(0, 6, coef_side, 0)

    def step(j, _):
        @pl.when(j < 6)
        def _():
            passing(lax.min(j, 5))

        @pl.when(jnp.logical_and(j > 2, j < 7))
        def _():
            loading(lax.max(lax.min(j - 1, 5), 0))

        @pl.when(jnp.logical_or(jnp.logical_and(j > 2, j < 5), j > 5))
        def _():
            finish(lax.max(j - 3 - j // 5, 0))

        return 0

    lax.fori_loop(2, 10, step, 0)

    def drain(j, _):
        for c in outs(j):
            c.wait()
        for d in range(chips):
            gather_copy(j, d).wait_send()
        for d in range(1, chips):
            forward_copy(j, d).wait_send()
        return 0

    lax.fori_loop(0, 6, drain, 0)


def solution(mesh):
    n_lat, n_lon = mesh.shape["lat"], mesh.shape["lon"]

    def per_device(*args):
        rows = args[0].shape[1]
        total = n_lat * rows
        ext = rows + 2 * TOP
        blocks = (rows + 2 * HALO) // BLOCK
        tiles = -(-len(FIELDS) * blocks // 16)
        chips = n_lat // 2
        vmem = lambda *shape: pltpu.VMEM(shape, jnp.float32)
        dma = lambda *shape: pltpu.SemaphoreType.DMA(shape)
        out = jax.ShapeDtypeStruct((12, rows, 128), jnp.float32)
        args = [pltpu.with_memory_space_constraint(a, pltpu.HBM) for a in args]
        return tuple(pl.pallas_call(
            functools.partial(kernel, n_lat, n_lon, rows),
            out_shape=[out] * 3,
            in_specs=[pl.BlockSpec(memory_space=pltpu.HBM)] * 9,
            out_specs=[pl.BlockSpec(memory_space=pl.ANY)] * 3,
            scratch_shapes=[
                vmem(12, rows, 128), vmem(12, rows, 128), pltpu.VMEM((rows, 128), jnp.int32), vmem(128, 128),
                vmem(ext, total), vmem(39, ext, 128), vmem(39, ext, 128), vmem(24, ext, 128), vmem(24, ext, 128),
                vmem(24, ext, 128), vmem(24, ext, 128), vmem(24, ext, 128), vmem(24, ext, 128),
                vmem(8, ext, 128), vmem(6, total, 256), vmem(2, ext, 128),
                vmem(tiles, BLOCK, 128), vmem(tiles, BLOCK, 128), vmem(tiles, BLOCK, 128),
                vmem(6, BLOCK, 128), vmem(6, BLOCK, 128), vmem(6, BLOCK, 128), vmem(12, rows, 128),
                dma(9), dma(6, chips), dma(6, chips), dma(6, chips - 1), dma(6, chips - 1),
                dma(4), dma(4), dma(2), dma(2), dma(6, 2), dma(6, 2), dma(6, 6),
            ],
            compiler_params=pltpu.CompilerParams(
                collective_id=0, has_side_effects=True, vmem_limit_bytes=48 * 1024 * 1024),
            cost_estimate=pl.CostEstimate(flops=1_000_000_000, bytes_accessed=6_000_000, transcendentals=0),
        )(*args))

    placed = (P(None, "lat", "lon"),) * 4 + (P("lat", "lon"),) * 3 + (P("lon", None), P("lat", "lon"))
    return jax.shard_map(
        per_device, mesh=mesh, in_specs=placed, out_specs=(P(None, "lat", "lon"),) * 3, check_vma=False)
```
